32 devices in a mesh: dp: 8 (over z, y), mp: 4 (over x, core).
Axes of the slice: x: 2, y: 2, z: 4, core: 2. Of those that a mesh axis runs over, the one named last changes fastest.
Arguments:
- seg_queries: bfloat16 [8, 256, 3072], P('dp', None, 'mp'), may hold values from -6 to 6
- seg_keys: bfloat16 [8, 256, 3072], P('dp', None, 'mp'), may hold values from -6 to 6
- seg_values: bfloat16 [8, 256, 3072], P('dp', None, 'mp'), may hold values from -8 to 8
- memory_keys: bfloat16 [8, 256, 3072], P('dp', None, 'mp'), may hold values from -4 to 4
- memory_values: bfloat16 [8, 256, 3072], P('dp', None, 'mp'), may hold values from -8 to 8
- new_owner: int32 [8], replicated, may hold values from 0 to 7, each once
- kept_blocks: int32 [8], replicated, may hold values from 1 to 2, 12 in all
- rel_bias: float32 [24, 512], P('mp'), may hold values from -5 to 5
- norm_gain: float32 [3072], P('mp'), may hold values from 0.5 to 1.5
- cotangent: bfloat16 [8, 256, 3072], P('dp', None, 'mp'), may hold values from -8 to 8
Outputs:
- attended: bfloat16 [8, 256, 3072], P('dp', None, 'mp')
- query_grad: bfloat16 [8, 256, 3072], P('dp', None, 'mp')
- key_grad: bfloat16 [8, 256, 3072], P('dp', None, 'mp')
- value_grad: bfloat16 [8, 256, 3072], P('dp', None, 'mp')
- bias_grad: float32 [24, 512], P('mp', 'dp')
- gain_grad: float32 [3072], P('mp')
The draws below stay inside these ranges and needn't reach their ends.
Inputs may be any that keep to these rules, and one draw needn't show every extreme that they name: `new_owner`: each old slot's stream goes to one device, and every device takes exactly one stream. A slot keeps its most recent kept_blocks blocks of 128 memory positions; some slot keeps all 2.
All inputs are finite; a program needn't handle non-finite values.
Results may differ from the reference program's by a relative error of at most 0.018.
Values may be sent and summed in bfloat16 or wider, within the bound.
A program may use at most 64 MiB of HBM per device.

```python
import math
import jax
import jax.numpy as jnp
import numpy as np
from jax import lax

HEADS = 24
DH = 128
SEG = 256
MEM = 256
BLOCK = 128
MEM_BLOCKS = 2
POS = 512
HD = 3072
STREAMS = 8
N_DP = 8


def base_field(key, shape):
    return jnp.clip(jax.random.normal(key, shape, jnp.float32), -4.0, 4.0)


def head_ramp():
    head_ids = (jnp.arange(HD) // DH).astype(jnp.float32)
    return 0.6 * 3.0 ** (head_ids / max(HEADS - 1, 1))


def draw_seg_queries(key, part):
    sample = base_field(jax.random.fold_in(key, 1), (STREAMS, SEG, HD))
    return sample.astype(jnp.bfloat16)


def draw_memory_keys(key, part):
    sample = base_field(jax.random.fold_in(key, 2), (STREAMS, MEM, HD))
    return sample.astype(jnp.bfloat16)


def draw_seg_values(key, part):
    sample = base_field(jax.random.fold_in(key, 3), (STREAMS, SEG, HD)) * head_ramp()
    return sample.astype(jnp.bfloat16)


def draw_memory_values(key, part):
    sample = base_field(jax.random.fold_in(key, 4), (STREAMS, MEM, HD)) * head_ramp()
    return sample.astype(jnp.bfloat16)


def draw_cotangent(key, part):
    stream_ids = jnp.arange(STREAMS).astype(jnp.float32)[:, None, None]
    sample = base_field(jax.random.fold_in(key, 5), (STREAMS, SEG, HD))
    factor = 0.5 * 3.0 ** (stream_ids / max(STREAMS - 1, 1))
    sample = sample * factor
    return sample.astype(jnp.bfloat16)


def levels(key, dims, split, low, largest):
    factor_of, own = 1.0, jax.random.fold_in(key, 6)
    for position, blocks in split:
        draws = jnp.exp(jax.random.uniform(jax.random.fold_in(own, position), (blocks,), jnp.float32, low / len(split), largest / len(split)))
        factor_of = factor_of * jnp.repeat(draws, dims[position] // blocks).reshape([-1 if axis == position else 1 for axis in range(len(dims))])
    return factor_of


def profile(number_of, total, limit, skew):
    weights = [(1 << 20) // math.isqrt(grade ** skew) + 1 for grade in range(2, number_of + 1)]
    surplus, given = total - limit - (number_of - 1), [1] * (number_of - 1)
    while surplus > 0:
        candidates = [i for i in range(number_of - 1) if given[i] < limit]
        pool, budget = sum([weights[i] for i in candidates]), surplus
        for i in candidates:
            addition = min(limit - given[i], max(1, budget * weights[i] // pool), surplus)
            given[i] = given[i] + addition
            surplus = surplus - addition
    return np.array([limit] + given)


def ragged_sizes(rng, amount, total, most, slope):
    if amount == 2:
        one = jax.random.randint(rng, (), max(1, total - most), min(most, total - 1) + 1)
        return jnp.stack([one, total - one])
    lengths = jnp.asarray(profile(amount, total, most, slope), jnp.int32)
    twos = (amount - 1) // 2
    donor, taker = lengths[1:1 + 2 * twos:2], lengths[2:2 + 2 * twos:2]
    room = jnp.minimum(donor - 1, most - taker)
    moved = jax.random.randint(jax.random.fold_in(rng, 1), (twos,), 0, 1 << 20) % (room + 1)
    lengths = lengths.at[1:1 + 2 * twos:2].set(donor - moved).at[2:2 + 2 * twos:2].set(taker + moved)
    return lengths[jax.random.permutation(jax.random.fold_in(rng, 2), amount)]


def gaussian(stream_key, shape, scale, most, cuts=(), kind=jnp.bfloat16):
    factor_of = levels(stream_key, shape, cuts, -0.22, 0.18) if cuts else 1.0
    values = jax.random.normal(stream_key, shape, jnp.float32) * scale * factor_of
    return jnp.minimum(jnp.maximum(values, -most), most).astype(kind)


def setup_inputs(seed: int = 0) -> dict:
    arg_keys = jax.random.split(jax.random.key(seed), 11)
    seg_queries = draw_seg_queries(jax.random.fold_in(arg_keys[10], 71), 0)
    seg_keys = gaussian(arg_keys[1], (STREAMS, SEG, HD), 1.0, 6.0, ((0, 8), (2, 4)))
    seg_values = draw_seg_values(jax.random.fold_in(arg_keys[10], 71), 0)
    memory_keys = draw_memory_keys(jax.random.fold_in(arg_keys[10], 71), 0)
    memory_values = draw_memory_values(jax.random.fold_in(arg_keys[10], 71), 0)
    new_owner = jax.random.permutation(arg_keys[5], STREAMS).astype(jnp.int32)
    kept_blocks = ragged_sizes(arg_keys[6], STREAMS, N_DP * (MEM_BLOCKS + 1) // 2, MEM_BLOCKS, 2).astype(jnp.int32)
    rel_bias = gaussian(arg_keys[7], (HEADS, POS), 1.0, 5.0, ((0, 4),), jnp.float32)
    norm_gain = jnp.clip(1.0 + 0.1 * jax.random.normal(arg_keys[8], (HD,), jnp.float32), 0.5, 1.5)
    cotangent = draw_cotangent(jax.random.fold_in(arg_keys[10], 71), 0)
    return {"seg_queries": seg_queries, "seg_keys": seg_keys, "seg_values": seg_values, "memory_keys": memory_keys, "memory_values": memory_values, "new_owner": new_owner, "kept_blocks": kept_blocks, "rel_bias": rel_bias, "norm_gain": norm_gain, "cotangent": cotangent}


def reference(seg_queries, seg_keys, seg_values, memory_keys, memory_values, new_owner, kept_blocks, rel_bias, norm_gain, cotangent):
    slot_ids = jnp.arange(STREAMS, dtype=jnp.int32)
    source = jnp.zeros((STREAMS,), jnp.int32).at[new_owner].set(slot_ids)
    score_scale = DH ** (-0.5)
    query_pos = jnp.arange(SEG, dtype=jnp.int32)[:, None]
    key_pos = jnp.arange(POS, dtype=jnp.int32)[None, :]
    distance = MEM + query_pos - key_pos
    dist_index = jnp.clip(distance, 0, POS - 1).astype(jnp.int32)
    bias_matrix = rel_bias[:, dist_index]

    def one_stream(stream):
        anchor = source[stream]
        kept_here = kept_blocks[anchor]
        query_heads = seg_queries[stream].astype(jnp.float32).reshape(SEG, HEADS, DH)
        key_heads = jnp.concatenate([memory_keys[anchor], seg_keys[stream]], axis=0).astype(jnp.float32).reshape(POS, HEADS, DH)
        value_heads = jnp.concatenate([memory_values[anchor], seg_values[stream]], axis=0).astype(jnp.float32).reshape(POS, HEADS, DH)
        allowed = (distance >= 0) & (key_pos >= MEM - BLOCK * kept_here)
        scores = jnp.einsum('ihd,jhd->hij', query_heads, key_heads) * score_scale + bias_matrix
        row_max = lax.optimization_barrier(jnp.max(jnp.where(allowed, scores, -1e+30), axis=-1, keepdims=True))
        unnormed = jnp.where(allowed, jnp.exp(scores - row_max), 0.0)
        weights_f = unnormed / lax.optimization_barrier(jnp.sum(unnormed, axis=-1, keepdims=True))
        weights_b = lax.optimization_barrier(weights_f.astype(jnp.bfloat16)).astype(jnp.float32)
        out_heads = jnp.einsum('hij,jhd->ihd', weights_b, value_heads)
        attn_out = out_heads.reshape(SEG, HD)
        inv_rms = lax.rsqrt(lax.optimization_barrier(jnp.sum(attn_out * attn_out, axis=1)) / HD + 1e-06)
        attended = (attn_out * inv_rms[:, None] * norm_gain).astype(jnp.bfloat16)
        upstream = cotangent[stream].astype(jnp.float32)
        gain_cot = upstream * norm_gain
        cross_sum = lax.optimization_barrier(jnp.sum(gain_cot * attn_out, axis=1))
        out_grad = (inv_rms[:, None] * gain_cot - attn_out * (inv_rms ** 3 * cross_sum / HD)[:, None]).astype(jnp.bfloat16)
        grad_heads = lax.optimization_barrier(out_grad).astype(jnp.float32).reshape(SEG, HEADS, DH)
        row_delta = jnp.einsum('ihd,ihd->hi', grad_heads, out_heads)
        prob_grad = jnp.einsum('ihd,jhd->hij', grad_heads, value_heads)
        score_grad = weights_f * (prob_grad - row_delta[:, :, None])
        score_grad_b = lax.optimization_barrier(score_grad.astype(jnp.bfloat16)).astype(jnp.float32)
        query_grad = (jnp.einsum('hij,jhd->ihd', score_grad_b, key_heads) * score_scale).reshape(SEG, HD).astype(jnp.bfloat16)
        key_grad = (jnp.einsum('hij,ihd->jhd', score_grad_b[:, :, MEM:], query_heads) * score_scale).reshape(SEG, HD).astype(jnp.bfloat16)
        value_grad = jnp.einsum('hij,ihd->jhd', weights_b[:, :, MEM:], grad_heads).reshape(SEG, HD).astype(jnp.bfloat16)
        local_bias = jnp.zeros((HEADS, POS), jnp.float32).at[:, dist_index].add(jnp.where(allowed, score_grad, 0.0))
        local_gain = lax.optimization_barrier(jnp.sum(upstream * attn_out * inv_rms[:, None], axis=0))
        return (attended, query_grad, key_grad, value_grad, local_bias, local_gain)
    results = lax.map(one_stream, slot_ids)
    return (results[0], results[1], results[2], results[3], lax.optimization_barrier(jnp.sum(results[4], axis=0)), lax.optimization_barrier(jnp.sum(results[5], axis=0)))
```

```python
import functools

import jax
import jax.numpy as jnp
from jax import lax
from jax.experimental import pallas as pl
from jax.experimental.pallas import tpu as pltpu
from jax.sharding import PartitionSpec as P

DH = 128
BLOCK = 128
HD = 3072
LANES = 128
MESH = pl.DeviceIdType.MESH
HIGHEST = lax.Precision.HIGHEST


def share_plan(n, mem_len, cols):
    col_groups = 1
    while n // col_groups > mem_len // 16 and col_groups < 2:
        col_groups *= 2
    members = min(n, (mem_len // 16) * col_groups)
    rows = mem_len // (members // col_groups)
    return members, rows, cols // col_groups, col_groups


def kernel(
    n,
    n_mp,
    plan,
    owner_ref,
    kept_ref,
    q_ref,
    k_ref,
    v_ref,
    mk_hbm,
    mv_hbm,
    bias_ref,
    gain_ref,
    cot_ref,
    att_ref,
    dq_ref,
    dk_ref,
    dv_ref,
    dbias_ref,
    dgain_ref,
    rx_k,
    rx_v,
    st_k,
    st_v,
    mem_k,
    mem_v,
    src_sm,
    prob,
    attn,
    mp_send,
    mp_recv,
    folded,
    diag,
    pkt,
    pkt_recv,
    p1_send,
    p1_recv,
    p2_send,
    p2_recv,
    mp_ssem,
    mp_rsem,
    dp_ssem,
    dp_rsem,
):
    members, rows, width, col_groups = plan
    me = lax.axis_index("dp")
    me_mp = lax.axis_index("mp")
    seg_len, cols = q_ref.shape
    mem_len = mem_k.shape[0]
    pos_len = mem_len + seg_len
    heads = cols // DH
    scale = DH ** (-0.5)
    every = members == n

    barrier = pltpu.get_barrier_semaphore()

    @pl.loop(1, n)
    def _(j):
        pl.semaphore_signal(
            barrier, inc=1, device_id={"dp": lax.rem(me + j, n)}, device_id_type=MESH
        )

    @pl.loop(1, n_mp)
    def _(j):
        pl.semaphore_signal(
            barrier, inc=1, device_id={"mp": lax.rem(me_mp + j, n_mp)}, device_id_type=MESH
        )

    pl.semaphore_wait(barrier, n - 1 + n_mp - 1)

    def guard(condition, run):
        if every:
            run()
        else:
            pl.when(condition)(run)

    def base(chunk):
        return 0 if every else chunk * members

    def is_member(chunk, device):
        return (device >= base(chunk)) & (device < base(chunk) + members)

    def window(ref, index):
        row = pl.multiple_of((index // col_groups) * rows, 16)
        if col_groups == 1:
            return ref.at[pl.ds(row, rows)]
        col = pl.multiple_of(lax.rem(index, col_groups) * width, LANES)
        return ref.at[pl.ds(row, rows), pl.ds(col, width)]

    chunks = ((mk_hbm, rx_k, st_k, mem_k), (mv_hbm, rx_v, st_v, mem_v))

    for c, (hbm, rx, st, mem) in enumerate(chunks):

        @pl.loop(1, n)
        def _(j):
            dest = lax.rem(me + j, n)

            def send():
                pltpu.make_async_remote_copy(
                    src_ref=window(hbm, dest - base(c)),
                    dst_ref=rx.at[me],
                    send_sem=p1_send.at[c],
                    recv_sem=p1_recv.at[c],
                    device_id={"dp": dest},
                    device_id_type=MESH,
                ).start()

            guard(is_member(c, dest), send)

        def own():
            pltpu.make_async_copy(
                window(hbm, me - base(c)), rx.at[me], p1_recv.at[c]
            ).start()

        guard(is_member(c, me), own)

    @pl.loop(0, n)
    def _(s):
        src_sm[s] = lax.fori_loop(
            0, n, lambda i, a: jnp.where(owner_ref[i] == s, i, a), jnp.int32(0)
        )

    kept_here = lax.fori_loop(
        0, n, lambda i, a: a + jnp.where(owner_ref[i] == me, kept_ref[i], 0), jnp.int32(0)
    )

    ki = lax.broadcasted_iota(jnp.int32, (pos_len, pos_len), 0)
    di = lax.broadcasted_iota(jnp.int32, (pos_len, pos_len), 1)
    total = ki + di
    flip = ((total == mem_len) | (total == mem_len + pos_len)).astype(jnp.float32)
    bias_pad = jnp.concatenate(
        [bias_ref[...], jnp.zeros((8 - heads, pos_len), jnp.float32)], axis=0
    )
    bias_rev = jnp.dot(bias_pad, flip, precision=HIGHEST, preferred_element_type=jnp.float32)

    qi = lax.broadcasted_iota(jnp.int32, (seg_len, seg_len), 0)
    ti = lax.broadcasted_iota(jnp.int32, (seg_len, seg_len), 1)
    causal = ti <= qi
    NT = (((1,), (1,)), ((), ()))
    TN = (((0,), (0,)), ((), ()))

    def cs(h):
        return slice(h * DH, (h + 1) * DH)

    def seg_scores(h):
        table = pltpu.roll(
            jnp.broadcast_to(bias_rev[h : h + 1], (seg_len, pos_len)),
            0,
            1,
            stride=1,
            stride_axis=0,
        )
        s = lax.dot_general(
            q_ref[:, cs(h)], k_ref[:, cs(h)], NT, preferred_element_type=jnp.float32
        )
        s = s * scale + table[:, mem_len:]
        prob[h, :, mem_len:] = jnp.where(causal, s, -1e30)
        prob[h, :, :mem_len] = table[:, :mem_len]

    def wait_first_and_forward(c):
        _, rx, st, mem = chunks[c]

        def run():
            pltpu.make_async_copy(rx, rx, p1_recv.at[c]).wait()

            @pl.loop(0, n)
            def _(s):
                st[s] = rx[src_sm[s]]

            @pl.loop(1, n)
            def _(j):
                dest = lax.rem(me + j, n)
                pltpu.make_async_remote_copy(
                    src_ref=st.at[dest],
                    dst_ref=window(mem, me - base(c)),
                    send_sem=p2_send.at[c],
                    recv_sem=p2_recv.at[c],
                    device_id={"dp": dest},
                    device_id_type=MESH,
                ).start()

            pltpu.make_async_copy(
                st.at[me], window(mem, me - base(c)), p2_recv.at[c]
            ).start()

        guard(is_member(c, me), run)

    for h in range(heads):
        seg_scores(h)
    wait_first_and_forward(0)
    wait_first_and_forward(1)
    pltpu.make_async_copy(mem_k, mem_k, p2_recv.at[0]).wait()

    mi = lax.broadcasted_iota(jnp.int32, (seg_len, mem_len), 1)
    live = mi >= mem_len - BLOCK * kept_here
    for h in range(heads):
        s_mem = lax.dot_general(
            q_ref[:, cs(h)], mem_k[:, cs(h)], NT, preferred_element_type=jnp.float32
        )
        s_mem = jnp.where(live, s_mem * scale + prob[h, :, :mem_len], -1e30)
        s_seg = prob[h, :, mem_len:]
        row_max = jnp.maximum(
            jnp.max(s_mem, axis=1, keepdims=True), jnp.max(s_seg, axis=1, keepdims=True)
        )
        e_mem = jnp.where(live, jnp.exp(s_mem - row_max), 0.0)
        e_seg = jnp.where(causal, jnp.exp(s_seg - row_max), 0.0)
        norm = 1.0 / (
            jnp.sum(e_mem, axis=1, keepdims=True) + jnp.sum(e_seg, axis=1, keepdims=True)
        )
        p_seg = e_seg * norm
        prob[h, :, :mem_len] = e_mem * norm
        prob[h, :, mem_len:] = p_seg
        attn[:, cs(h)] = jnp.dot(
            p_seg.astype(jnp.bfloat16), v_ref[:, cs(h)], preferred_element_type=jnp.float32
        )

    pltpu.make_async_copy(mem_v, mem_v, p2_recv.at[1]).wait()

    squares = jnp.zeros((seg_len, DH), jnp.float32)
    crosses = jnp.zeros((seg_len, DH), jnp.float32)
    for h in range(heads):
        out = attn[:, cs(h)] + jnp.dot(
            prob[h, :, :mem_len].astype(jnp.bfloat16),
            mem_v[:, cs(h)],
            preferred_element_type=jnp.float32,
        )
        attn[:, cs(h)] = out
        squares = squares + out * out
        crosses = crosses + cot_ref[:, cs(h)].astype(jnp.float32) * gain_ref[:, cs(h)] * out
    lane = lax.broadcasted_iota(jnp.int32, (seg_len, DH), 1)
    both = jnp.where(
        lane == 0,
        jnp.sum(squares, axis=1, keepdims=True),
        jnp.sum(crosses, axis=1, keepdims=True),
    )
    mp_send[...] = jnp.transpose(both)[:8]

    @pl.loop(1, n_mp)
    def _(j):
        pltpu.make_async_remote_copy(
            src_ref=mp_send,
            dst_ref=mp_recv.at[me_mp],
            send_sem=mp_ssem,
            recv_sem=mp_rsem,
            device_id={"mp": lax.rem(me_mp + j, n_mp)},
            device_id_type=MESH,
        ).start()

    pltpu.make_async_copy(mp_send, mp_recv.at[me_mp], mp_rsem).start()
    pltpu.make_async_copy(mp_recv, mp_recv, mp_rsem).wait()
    sums = mp_recv[0]
    for m in range(1, n_mp):
        sums = sums + mp_recv[m]
    sums = jnp.transpose(
        jnp.concatenate([sums, jnp.zeros((LANES - 8, seg_len), jnp.float32)], axis=0)
    )
    inv_rms = lax.rsqrt(sums[:, 0:1] / HD + 1e-06)
    pull = inv_rms * inv_rms * inv_rms * sums[:, 1:2] / HD

    gain_rows = []
    for h in range(heads):
        out = attn[:, cs(h)]
        gain = gain_ref[:, cs(h)]
        up = cot_ref[:, cs(h)].astype(jnp.float32)
        normed = out * inv_rms
        att_ref[:, cs(h)] = (normed * gain).astype(jnp.bfloat16)
        gain_rows.append(jnp.sum(up * normed, axis=0, keepdims=True))
        og = (inv_rms * (up * gain) - out * pull).astype(jnp.bfloat16)
        delta = jnp.sum(og.astype(jnp.float32) * out, axis=1, keepdims=True)
        p_mem = prob[h, :, :mem_len]
        p_seg = prob[h, :, mem_len:]
        g_mem = p_mem * (
            lax.dot_general(og, mem_v[:, cs(h)], NT, preferred_element_type=jnp.float32) - delta
        )
        g_seg = p_seg * (
            lax.dot_general(og, v_ref[:, cs(h)], NT, preferred_element_type=jnp.float32) - delta
        )
        gb_mem = g_mem.astype(jnp.bfloat16)
        gb_seg = g_seg.astype(jnp.bfloat16)
        dq = jnp.dot(gb_mem, mem_k[:, cs(h)], preferred_element_type=jnp.float32) + jnp.dot(
            gb_seg, k_ref[:, cs(h)], preferred_element_type=jnp.float32
        )
        dq_ref[:, cs(h)] = (dq * scale).astype(jnp.bfloat16)
        dk = lax.dot_general(gb_seg, q_ref[:, cs(h)], TN, preferred_element_type=jnp.float32)
        dk_ref[:, cs(h)] = (dk * scale).astype(jnp.bfloat16)
        dv = lax.dot_general(
            p_seg.astype(jnp.bfloat16), og, TN, preferred_element_type=jnp.float32
        )
        dv_ref[:, cs(h)] = dv.astype(jnp.bfloat16)
        x = jnp.concatenate([g_mem, g_seg], axis=1)
        half = seg_len // 2
        while half >= 8:
            x = x[:half] + pltpu.roll(x[half:], pos_len - half, 1)
            half //= 2
        folded[h * 8 : (h + 1) * 8] = x

    x = folded[...]
    for half in (4, 2, 1):
        x = x + pltpu.roll(pltpu.roll(x, pos_len - half, 1), heads * 8 - half, 0)
    rows8 = [x[8 * h : 8 * h + 1] for h in range(heads)]
    rows8.append(jnp.zeros((8 - heads, pos_len), jnp.float32))
    diag[...] = jnp.dot(
        jnp.concatenate(rows8, axis=0), flip, precision=HIGHEST, preferred_element_type=jnp.float32
    )
    gain_block = jnp.concatenate(
        gain_rows + [jnp.zeros((8 - heads, DH), jnp.float32)], axis=0
    )
    for b in range(pos_len // LANES):
        pkt[b, :8] = diag[:, b * LANES : (b + 1) * LANES]
        pkt[b, 8:] = gain_block

    part = pos_len // n

    @pl.loop(1, n)
    def _(j):
        dest = lax.rem(me + j, n)
        pltpu.make_async_remote_copy(
            src_ref=pkt.at[(dest * part) // LANES],
            dst_ref=pkt_recv.at[me],
            send_sem=dp_ssem,
            recv_sem=dp_rsem,
            device_id={"dp": dest},
            device_id_type=MESH,
        ).start()

    pltpu.make_async_copy(pkt.at[(me * part) // LANES], pkt_recv.at[me], dp_rsem).start()

    for c, (hbm, rx, st, mem) in enumerate(chunks):

        def wait_p1(count):
            pltpu.make_async_copy(
                rx.at[pl.ds(0, count)], rx.at[pl.ds(0, count)], p1_send.at[c]
            ).wait()

        def wait_p2():
            pltpu.make_async_copy(
                st.at[pl.ds(0, n - 1)], st.at[pl.ds(0, n - 1)], p2_send.at[c]
            ).wait()

        guard(is_member(c, me), functools.partial(wait_p1, members - 1))
        if not every:
            pl.when(jnp.logical_not(is_member(c, me)))(functools.partial(wait_p1, members))
        guard(is_member(c, me), wait_p2)
    pltpu.make_async_copy(
        mp_recv.at[pl.ds(0, n_mp - 1)], mp_recv.at[pl.ds(0, n_mp - 1)], mp_ssem
    ).wait()

    pltpu.make_async_copy(pkt_recv, pkt_recv, dp_rsem).wait()
    acc = pkt_recv[0]
    for s in range(1, n):
        acc = acc + pkt_recv[s]
    offset = lax.rem(me * part, LANES)
    mine = pltpu.roll(acc[:8], lax.rem(LANES - offset, LANES), 1)
    dbias_ref[...] = mine[:heads, :part]
    for h in range(heads):
        dgain_ref[:, cs(h)] = acc[8 + h : 9 + h]
    pltpu.make_async_copy(
        pkt_recv.at[pl.ds(0, n - 1)], pkt_recv.at[pl.ds(0, n - 1)], dp_ssem
    ).wait()


def body(
    n,
    n_mp,
    seg_queries,
    seg_keys,
    seg_values,
    memory_keys,
    memory_values,
    new_owner,
    kept_blocks,
    rel_bias,
    norm_gain,
    cotangent,
):
    _, seg_len, cols = seg_queries.shape
    mem_len = memory_keys.shape[1]
    heads, pos_len = rel_bias.shape
    part = pos_len // n
    plan = share_plan(n, mem_len, cols)
    members, rows, width, _ = plan
    bf16, f32 = jnp.bfloat16, jnp.float32
    vmem = pl.BlockSpec(memory_space=pltpu.VMEM)
    smem = pl.BlockSpec(memory_space=pltpu.SMEM)
    hbm = pl.BlockSpec(memory_space=pl.ANY)
    big = jax.ShapeDtypeStruct((seg_len, cols), bf16)
    outs = pl.pallas_call(
        functools.partial(kernel, n, n_mp, plan),
        out_shape=(
            big,
            big,
            big,
            big,
            jax.ShapeDtypeStruct((heads, part), f32),
            jax.ShapeDtypeStruct((1, cols), f32),
        ),
        in_specs=[smem, smem, vmem, vmem, vmem, hbm, hbm, vmem, vmem, vmem],
        out_specs=(vmem,) * 6,
        scratch_shapes=[
            pltpu.VMEM((n, rows, width), bf16),
            pltpu.VMEM((n, rows, width), bf16),
            pltpu.VMEM((n, rows, width), bf16),
            pltpu.VMEM((n, rows, width), bf16),
            pltpu.VMEM((mem_len, cols), bf16),
            pltpu.VMEM((mem_len, cols), bf16),
            pltpu.SMEM((n,), jnp.int32),
            pltpu.VMEM((heads, seg_len, pos_len), f32),
            pltpu.VMEM((seg_len, cols), f32),
            pltpu.VMEM((8, seg_len), f32),
            pltpu.VMEM((n_mp, 8, seg_len), f32),
            pltpu.VMEM((heads * 8, pos_len), f32),
            pltpu.VMEM((8, pos_len), f32),
            pltpu.VMEM((pos_len // LANES, 16, LANES), f32),
            pltpu.VMEM((n, 16, LANES), f32),
            pltpu.SemaphoreType.DMA((2,)),
            pltpu.SemaphoreType.DMA((2,)),
            pltpu.SemaphoreType.DMA((2,)),
            pltpu.SemaphoreType.DMA((2,)),
            pltpu.SemaphoreType.DMA,
            pltpu.SemaphoreType.DMA,
            pltpu.SemaphoreType.DMA,
            pltpu.SemaphoreType.DMA,
        ],
        compiler_params=pltpu.CompilerParams(
            collective_id=0, has_side_effects=True, vmem_limit_bytes=40 * 1024 * 1024
        ),
    )(
        new_owner,
        kept_blocks,
        seg_queries[0],
        seg_keys[0],
        seg_values[0],
        memory_keys[0],
        memory_values[0],
        rel_bias,
        norm_gain[None],
        cotangent[0],
    )
    return (
        outs[0][None],
        outs[1][None],
        outs[2][None],
        outs[3][None],
        outs[4],
        outs[5][0],
    )


def solution(mesh):
    rows = P("dp", None, "mp")
    in_specs = (rows, rows, rows, rows, rows, P(), P(), P("mp", None), P("mp"), rows)
    out_specs = (rows, rows, rows, rows, P("mp", "dp"), P("mp"))
    return jax.shard_map(
        functools.partial(body, mesh.shape["dp"], mesh.shape["mp"]),
        mesh=mesh,
        in_specs=in_specs,
        out_specs=out_specs,
        check_vma=False,
    )
```

```python
import functools

import jax
import jax.numpy as jnp
from jax import lax
from jax.experimental import pallas as pl
from jax.experimental.pallas import tpu as pltpu
from jax.sharding import PartitionSpec as P

DH = 128
BLOCK = 128
HD = 3072
LANES = 128
MESH = pl.DeviceIdType.MESH
HIGHEST = lax.Precision.HIGHEST


def share_plan(n, mem_len, cols):
    col_groups = 1
    while n // col_groups > mem_len // 16 and col_groups < 2:
        col_groups *= 2
    members = min(n, (mem_len // 16) * col_groups)
    rows = mem_len // (members // col_groups)
    return members, rows, cols // col_groups, col_groups


def kernel(
    n,
    n_mp,
    plan,
    owner_ref,
    kept_ref,
    q_hbm,
    k_hbm,
    v_hbm,
    mk_hbm,
    mv_hbm,
    bias_hbm,
    gain_ref,
    cot_hbm,
    att_hbm,
    dq_hbm,
    dk_hbm,
    dv_hbm,
    dbias_ref,
    dgain_ref,
    q_ref,
    k_ref,
    v_ref,
    bias_ref,
    cot_ref,
    att_ref,
    dq_ref,
    dk_ref,
    dv_ref,
    grads,
    in_sem,
    out_sem,
    rx_k,
    rx_v,
    st_k,
    st_v,
    mem_k,
    mem_v,
    src_sm,
    prob,
    attn,
    mp_send,
    mp_recv,
    folded,
    diag,
    pkt,
    pkt_recv,
    p1_send,
    p1_recv,
    p2_send,
    p2_recv,
    mp_ssem,
    mp_rsem,
    dp_ssem,
    dp_rsem,
):
    members, rows, width, col_groups = plan
    me = lax.axis_index("dp")
    me_mp = lax.axis_index("mp")
    seg_len, cols = q_ref.shape
    mem_len = mem_k.shape[0]
    pos_len = mem_len + seg_len
    heads = cols // DH
    scale = DH ** (-0.5)
    every = members == n

    loads = [
        pltpu.make_async_copy(a, b, in_sem.at[i])
        for i, (a, b) in enumerate(
            (
                (bias_hbm, bias_ref),
                (q_hbm, q_ref),
                (k_hbm, k_ref),
                (v_hbm, v_ref),
                (cot_hbm, cot_ref),
            )
        )
    ]
    barrier = pltpu.get_barrier_semaphore()

    @pl.loop(1, n)
    def _(j):
        pl.semaphore_signal(
            barrier, inc=1, device_id={"dp": lax.rem(me + j, n)}, device_id_type=MESH
        )

    @pl.loop(1, n_mp)
    def _(j):
        pl.semaphore_signal(
            barrier, inc=1, device_id={"mp": lax.rem(me_mp + j, n_mp)}, device_id_type=MESH
        )

    pl.semaphore_wait(barrier, n - 1 + n_mp - 1)

    def guard(condition, run):
        if every:
            run()
        else:
            pl.when(condition)(run)

    def base(chunk):
        return 0 if every else chunk * members

    def is_member(chunk, device):
        return (device >= base(chunk)) & (device < base(chunk) + members)

    def window(ref, index):
        row = pl.multiple_of((index // col_groups) * rows, 16)
        if col_groups == 1:
            return ref.at[pl.ds(row, rows)]
        col = pl.multiple_of(lax.rem(index, col_groups) * width, LANES)
        return ref.at[pl.ds(row, rows), pl.ds(col, width)]

    chunks = ((mk_hbm, rx_k, st_k, mem_k), (mv_hbm, rx_v, st_v, mem_v))

    for c, (hbm, rx, st, mem) in enumerate(chunks):

        @pl.loop(1, n)
        def _(j):
            dest = lax.rem(me + j, n)

            def send():
                pltpu.make_async_remote_copy(
                    src_ref=window(hbm, dest - base(c)),
                    dst_ref=rx.at[me],
                    send_sem=p1_send.at[c],
                    recv_sem=p1_recv.at[c],
                    device_id={"dp": dest},
                    device_id_type=MESH,
                ).start()

            guard(is_member(c, dest), send)

        def own():
            pltpu.make_async_copy(
                window(hbm, me - base(c)), rx.at[me], p1_recv.at[c]
            ).start()

        guard(is_member(c, me), own)

    for load in loads:
        load.start()

    @pl.loop(0, n)
    def _(s):
        src_sm[s] = lax.fori_loop(
            0, n, lambda i, a: jnp.where(owner_ref[i] == s, i, a), jnp.int32(0)
        )

    kept_here = lax.fori_loop(
        0, n, lambda i, a: a + jnp.where(owner_ref[i] == me, kept_ref[i], 0), jnp.int32(0)
    )

    loads[0].wait()
    ki = lax.broadcasted_iota(jnp.int32, (pos_len, pos_len), 0)
    di = lax.broadcasted_iota(jnp.int32, (pos_len, pos_len), 1)
    total = ki + di
    flip = ((total == mem_len) | (total == mem_len + pos_len)).astype(jnp.float32)
    bias_pad = jnp.concatenate(
        [bias_ref[...], jnp.zeros((8 - heads, pos_len), jnp.float32)], axis=0
    )
    bias_rev = jnp.dot(bias_pad, flip, precision=HIGHEST, preferred_element_type=jnp.float32)

    qi = lax.broadcasted_iota(jnp.int32, (seg_len, seg_len), 0)
    ti = lax.broadcasted_iota(jnp.int32, (seg_len, seg_len), 1)
    causal = ti <= qi
    NT = (((1,), (1,)), ((), ()))
    TN = (((0,), (0,)), ((), ()))

    def cs(h):
        return slice(h * DH, (h + 1) * DH)

    def seg_scores(h):
        table = pltpu.roll(
            jnp.broadcast_to(bias_rev[h : h + 1], (seg_len, pos_len)),
            0,
            1,
            stride=1,
            stride_axis=0,
        )
        s = lax.dot_general(
            q_ref[:, cs(h)], k_ref[:, cs(h)], NT, preferred_element_type=jnp.float32
        )
        s = s * scale + table[:, mem_len:]
        prob[h, :, mem_len:] = jnp.where(causal, s, -1e30)
        prob[h, :, :mem_len] = table[:, :mem_len]

    def wait_first_and_forward(c):
        _, rx, st, mem = chunks[c]

        def run():
            pltpu.make_async_copy(rx, rx, p1_recv.at[c]).wait()

            @pl.loop(0, n)
            def _(s):
                st[s] = rx[src_sm[s]]

            @pl.loop(1, n)
            def _(j):
                dest = lax.rem(me + j, n)
                pltpu.make_async_remote_copy(
                    src_ref=st.at[dest],
                    dst_ref=window(mem, me - base(c)),
                    send_sem=p2_send.at[c],
                    recv_sem=p2_recv.at[c],
                    device_id={"dp": dest},
                    device_id_type=MESH,
                ).start()

            pltpu.make_async_copy(
                st.at[me], window(mem, me - base(c)), p2_recv.at[c]
            ).start()

        guard(is_member(c, me), run)

    for load in loads[1:]:
        load.wait()
    for h in range(heads):
        seg_scores(h)
    wait_first_and_forward(0)
    wait_first_and_forward(1)
    pltpu.make_async_copy(mem_k, mem_k, p2_recv.at[0]).wait()

    mi = lax.broadcasted_iota(jnp.int32, (seg_len, mem_len), 1)
    live = mi >= mem_len - BLOCK * kept_here
    for h in range(heads):
        s_mem = lax.dot_general(
            q_ref[:, cs(h)], mem_k[:, cs(h)], NT, preferred_element_type=jnp.float32
        )
        s_mem = jnp.where(live, s_mem * scale + prob[h, :, :mem_len], -1e30)
        s_seg = prob[h, :, mem_len:]
        row_max = jnp.maximum(
            jnp.max(s_mem, axis=1, keepdims=True), jnp.max(s_seg, axis=1, keepdims=True)
        )
        e_mem = jnp.where(live, jnp.exp(s_mem - row_max), 0.0)
        e_seg = jnp.where(causal, jnp.exp(s_seg - row_max), 0.0)
        norm = 1.0 / (
            jnp.sum(e_mem, axis=1, keepdims=True) + jnp.sum(e_seg, axis=1, keepdims=True)
        )
        p_seg = e_seg * norm
        prob[h, :, :mem_len] = e_mem * norm
        prob[h, :, mem_len:] = p_seg
        attn[:, cs(h)] = jnp.dot(
            p_seg.astype(jnp.bfloat16), v_ref[:, cs(h)], preferred_element_type=jnp.float32
        )

    pltpu.make_async_copy(mem_v, mem_v, p2_recv.at[1]).wait()

    squares = jnp.zeros((seg_len, DH), jnp.float32)
    crosses = jnp.zeros((seg_len, DH), jnp.float32)
    for h in range(heads):
        out = attn[:, cs(h)] + jnp.dot(
            prob[h, :, :mem_len].astype(jnp.bfloat16),
            mem_v[:, cs(h)],
            preferred_element_type=jnp.float32,
        )
        attn[:, cs(h)] = out
        squares = squares + out * out
        crosses = crosses + cot_ref[:, cs(h)].astype(jnp.float32) * gain_ref[cs(h)][None] * out
    lane = lax.broadcasted_iota(jnp.int32, (seg_len, DH), 1)
    both = jnp.where(
        lane == 0,
        jnp.sum(squares, axis=1, keepdims=True),
        jnp.sum(crosses, axis=1, keepdims=True),
    )
    mp_send[...] = jnp.transpose(both)[:8]

    @pl.loop(1, n_mp)
    def _(j):
        pltpu.make_async_remote_copy(
            src_ref=mp_send,
            dst_ref=mp_recv.at[me_mp],
            send_sem=mp_ssem,
            recv_sem=mp_rsem,
            device_id={"mp": lax.rem(me_mp + j, n_mp)},
            device_id_type=MESH,
        ).start()

    pltpu.make_async_copy(mp_send, mp_recv.at[me_mp], mp_rsem).start()
    pltpu.make_async_copy(mp_recv, mp_recv, mp_rsem).wait()
    sums = mp_recv[0]
    for m in range(1, n_mp):
        sums = sums + mp_recv[m]
    sums = jnp.transpose(
        jnp.concatenate([sums, jnp.zeros((LANES - 8, seg_len), jnp.float32)], axis=0)
    )
    inv_rms = lax.rsqrt(sums[:, 0:1] / HD + 1e-06)
    pull = inv_rms * inv_rms * inv_rms * sums[:, 1:2] / HD

    gain_rows, out_grads = [], []
    for h in range(heads):
        out = attn[:, cs(h)]
        gain = gain_ref[cs(h)][None]
        up = cot_ref[:, cs(h)].astype(jnp.float32)
        normed = out * inv_rms
        att_ref[:, cs(h)] = (normed * gain).astype(jnp.bfloat16)
        gain_rows.append(jnp.sum(up * normed, axis=0, keepdims=True))
        og = (inv_rms * (up * gain) - out * pull).astype(jnp.bfloat16)
        delta = jnp.sum(og.astype(jnp.float32) * out, axis=1, keepdims=True)
        p_mem = prob[h, :, :mem_len]
        p_seg = prob[h, :, mem_len:]
        g_mem = p_mem * (
            lax.dot_general(og, mem_v[:, cs(h)], NT, preferred_element_type=jnp.float32) - delta
        )
        g_seg = p_seg * (
            lax.dot_general(og, v_ref[:, cs(h)], NT, preferred_element_type=jnp.float32) - delta
        )
        grads[h, :, :mem_len] = g_mem.astype(jnp.bfloat16)
        grads[h, :, mem_len:] = g_seg.astype(jnp.bfloat16)
        out_grads.append(og)
        x = jnp.concatenate([g_mem, g_seg], axis=1)
        half = seg_len // 2
        while half >= 8:
            x = x[:half] + pltpu.roll(x[half:], pos_len - half, 1)
            half //= 2
        folded[h * 8 : (h + 1) * 8] = x

    x = folded[...]
    for half in (4, 2, 1):
        x = x + pltpu.roll(pltpu.roll(x, pos_len - half, 1), heads * 8 - half, 0)
    rows8 = [x[8 * h : 8 * h + 1] for h in range(heads)]
    rows8.append(jnp.zeros((8 - heads, pos_len), jnp.float32))
    diag[...] = jnp.dot(
        jnp.concatenate(rows8, axis=0), flip, precision=HIGHEST, preferred_element_type=jnp.float32
    )
    gain_block = jnp.concatenate(
        gain_rows + [jnp.zeros((8 - heads, DH), jnp.float32)], axis=0
    )
    for b in range(pos_len // LANES):
        pkt[b, :8] = diag[:, b * LANES : (b + 1) * LANES]
        pkt[b, 8:] = gain_block

    part = pos_len // n

    @pl.loop(1, n)
    def _(j):
        dest = lax.rem(me + j, n)
        pltpu.make_async_remote_copy(
            src_ref=pkt.at[(dest * part) // LANES],
            dst_ref=pkt_recv.at[me],
            send_sem=dp_ssem,
            recv_sem=dp_rsem,
            device_id={"dp": dest},
            device_id_type=MESH,
        ).start()

    pltpu.make_async_copy(pkt.at[(me * part) // LANES], pkt_recv.at[me], dp_rsem).start()

    stores = [
        pltpu.make_async_copy(a, b, out_sem.at[i])
        for i, (a, b) in enumerate(
            ((att_ref, att_hbm), (dv_ref, dv_hbm), (dk_ref, dk_hbm), (dq_ref, dq_hbm))
        )
    ]
    stores[0].start()
    for h in range(heads):
        dv = lax.dot_general(
            prob[h, :, mem_len:].astype(jnp.bfloat16),
            out_grads[h],
            TN,
            preferred_element_type=jnp.float32,
        )
        dv_ref[:, cs(h)] = dv.astype(jnp.bfloat16)
    stores[1].start()
    for h in range(heads):
        dk = lax.dot_general(
            grads[h, :, mem_len:], q_ref[:, cs(h)], TN, preferred_element_type=jnp.float32
        )
        dk_ref[:, cs(h)] = (dk * scale).astype(jnp.bfloat16)
    stores[2].start()
    for h in range(heads):
        dq = jnp.dot(
            grads[h, :, :mem_len], mem_k[:, cs(h)], preferred_element_type=jnp.float32
        ) + jnp.dot(grads[h, :, mem_len:], k_ref[:, cs(h)], preferred_element_type=jnp.float32)
        dq_ref[:, cs(h)] = (dq * scale).astype(jnp.bfloat16)
    stores[3].start()

    for c, (hbm, rx, st, mem) in enumerate(chunks):

        def wait_p1(count):
            pltpu.make_async_copy(
                rx.at[pl.ds(0, count)], rx.at[pl.ds(0, count)], p1_send.at[c]
            ).wait()

        def wait_p2():
            pltpu.make_async_copy(
                st.at[pl.ds(0, n - 1)], st.at[pl.ds(0, n - 1)], p2_send.at[c]
            ).wait()

        guard(is_member(c, me), functools.partial(wait_p1, members - 1))
        if not every:
            pl.when(jnp.logical_not(is_member(c, me)))(functools.partial(wait_p1, members))
        guard(is_member(c, me), wait_p2)
    pltpu.make_async_copy(
        mp_recv.at[pl.ds(0, n_mp - 1)], mp_recv.at[pl.ds(0, n_mp - 1)], mp_ssem
    ).wait()

    pltpu.make_async_copy(pkt_recv, pkt_recv, dp_rsem).wait()
    acc = pkt_recv[0]
    for s in range(1, n):
        acc = acc + pkt_recv[s]
    offset = lax.rem(me * part, LANES)
    mine = pltpu.roll(acc[:8], lax.rem(LANES - offset, LANES), 1)
    dbias_ref[...] = mine[:heads, :part]
    for h in range(heads):
        dgain_ref[cs(h)] = acc[8 + h]
    for store in stores:
        store.wait()
    pltpu.make_async_copy(
        pkt_recv.at[pl.ds(0, n - 1)], pkt_recv.at[pl.ds(0, n - 1)], dp_ssem
    ).wait()


def hand_on(*refs):
    count = len(refs) // 2
    sem = refs[-1]
    copies = [
        pltpu.make_async_copy(refs[i], refs[count + i], sem.at[i]) for i in range(count)
    ]
    for copy in copies:
        copy.start()
    for copy in copies:
        copy.wait()


def body(
    n,
    n_mp,
    seg_queries,
    seg_keys,
    seg_values,
    memory_keys,
    memory_values,
    new_owner,
    kept_blocks,
    rel_bias,
    norm_gain,
    cotangent,
):
    _, seg_len, cols = seg_queries.shape
    mem_len = memory_keys.shape[1]
    heads, pos_len = rel_bias.shape
    part = pos_len // n
    plan = share_plan(n, mem_len, cols)
    members, rows, width, _ = plan
    bf16, f32 = jnp.bfloat16, jnp.float32
    vmem = pl.BlockSpec(memory_space=pltpu.VMEM)
    smem = pl.BlockSpec(memory_space=pltpu.SMEM)
    hbm = pl.BlockSpec(memory_space=pl.ANY)
    big = jax.ShapeDtypeStruct((seg_len, cols), bf16)
    outs = pl.pallas_call(
        functools.partial(kernel, n, n_mp, plan),
        out_shape=(
            big,
            big,
            big,
            big,
            jax.ShapeDtypeStruct((heads, part), f32),
            jax.ShapeDtypeStruct((cols,), f32),
        ),
        in_specs=[smem, smem, hbm, hbm, hbm, hbm, hbm, hbm, vmem, hbm],
        out_specs=(hbm,) * 4 + (vmem,) * 2,
        scratch_shapes=[
            pltpu.VMEM((seg_len, cols), bf16),
            pltpu.VMEM((seg_len, cols), bf16),
            pltpu.VMEM((seg_len, cols), bf16),
            pltpu.VMEM((heads, pos_len), f32),
            pltpu.VMEM((seg_len, cols), bf16),
            pltpu.VMEM((seg_len, cols), bf16),
            pltpu.VMEM((seg_len, cols), bf16),
            pltpu.VMEM((seg_len, cols), bf16),
            pltpu.VMEM((seg_len, cols), bf16),
            pltpu.VMEM((heads, seg_len, pos_len), bf16),
            pltpu.SemaphoreType.DMA((5,)),
            pltpu.SemaphoreType.DMA((4,)),
            pltpu.VMEM((n, rows, width), bf16),
            pltpu.VMEM((n, rows, width), bf16),
            pltpu.VMEM((n, rows, width), bf16),
            pltpu.VMEM((n, rows, width), bf16),
            pltpu.VMEM((mem_len, cols), bf16),
            pltpu.VMEM((mem_len, cols), bf16),
            pltpu.SMEM((n,), jnp.int32),
            pltpu.VMEM((heads, seg_len, pos_len), f32),
            pltpu.VMEM((seg_len, cols), f32),
            pltpu.VMEM((8, seg_len), f32),
            pltpu.VMEM((n_mp, 8, seg_len), f32),
            pltpu.VMEM((heads * 8, pos_len), f32),
            pltpu.VMEM((8, pos_len), f32),
            pltpu.VMEM((pos_len // LANES, 16, LANES), f32),
            pltpu.VMEM((n, 16, LANES), f32),
            pltpu.SemaphoreType.DMA((2,)),
            pltpu.SemaphoreType.DMA((2,)),
            pltpu.SemaphoreType.DMA((2,)),
            pltpu.SemaphoreType.DMA((2,)),
            pltpu.SemaphoreType.DMA,
            pltpu.SemaphoreType.DMA,
            pltpu.SemaphoreType.DMA,
            pltpu.SemaphoreType.DMA,
        ],
        compiler_params=pltpu.CompilerParams(
            collective_id=0, has_side_effects=True, vmem_limit_bytes=60 * 1024 * 1024
        ),
    )(
        new_owner,
        kept_blocks,
        seg_queries[0],
        seg_keys[0],
        seg_values[0],
        memory_keys[0],
        memory_values[0],
        rel_bias,
        norm_gain,
        cotangent[0],
    )
    final = pl.pallas_call(
        hand_on,
        out_shape=tuple(jax.ShapeDtypeStruct(o.shape, o.dtype) for o in outs),
        in_specs=[hbm] * 6,
        out_specs=(hbm,) * 6,
        scratch_shapes=[pltpu.SemaphoreType.DMA((6,))],
        compiler_params=pltpu.CompilerParams(vmem_limit_bytes=60 * 1024 * 1024),
    )(*outs)
    return (
        final[0][None],
        final[1][None],
        final[2][None],
        final[3][None],
        final[4],
        final[5],
    )


def solution(mesh):
    rows = P("dp", None, "mp")
    in_specs = (rows, rows, rows, rows, rows, P(), P(), P("mp", None), P("mp"), rows)
    out_specs = (rows, rows, rows, rows, P("mp", "dp"), P("mp"))
    return jax.shard_map(
        functools.partial(body, mesh.shape["dp"], mesh.shape["mp"]),
        mesh=mesh,
        in_specs=in_specs,
        out_specs=out_specs,
        check_vma=False,
    )
```

```python
import functools

import jax
import jax.numpy as jnp
from jax import lax
from jax.experimental import pallas as pl
from jax.experimental.pallas import tpu as pltpu
from jax.sharding import PartitionSpec as P

DH = 128
BLOCK = 128
HD = 3072
LANES = 128
MESH = pl.DeviceIdType.MESH
HIGHEST = lax.Precision.HIGHEST


def share_plan(n, mem_len, cols):
    col_groups = 1
    while n // col_groups > mem_len // 16 and col_groups < 2:
        col_groups *= 2
    members = min(n, (mem_len // 16) * col_groups)
    rows = mem_len // (members // col_groups)
    return members, rows, cols // col_groups, col_groups


def kernel(
    n,
    n_mp,
    plan,
    owner_hbm,
    kept_hbm,
    q_hbm,
    k_hbm,
    v_hbm,
    mk_hbm,
    mv_hbm,
    bias_hbm,
    gain_hbm,
    cot_hbm,
    att_hbm,
    dq_hbm,
    dk_hbm,
    dv_hbm,
    dbias_ref,
    dgain_ref,
    q_ref,
    k_ref,
    v_ref,
    bias_ref,
    cot_ref,
    gain_ref,
    owner_ref,
    kept_ref,
    att_ref,
    dq_ref,
    dk_ref,
    dv_ref,
    grads,
    in_sem,
    out_sem,
    rx_k,
    rx_v,
    st_k,
    st_v,
    mem_k,
    mem_v,
    src_sm,
    prob,
    attn,
    mp_send,
    mp_recv,
    folded,
    diag,
    pkt,
    pkt_recv,
    p1_send,
    p1_recv,
    p2_send,
    p2_recv,
    mp_ssem,
    mp_rsem,
    dp_ssem,
    dp_rsem,
):
    members, rows, width, col_groups = plan
    me = lax.axis_index("dp")
    me_mp = lax.axis_index("mp")
    seg_len, cols = q_ref.shape
    mem_len = mem_k.shape[0]
    pos_len = mem_len + seg_len
    heads = cols // DH
    scale = DH ** (-0.5)
    every = members == n

    loads = [
        pltpu.make_async_copy(a, b, in_sem.at[i])
        for i, (a, b) in enumerate(
            (
                (owner_hbm, owner_ref),
                (kept_hbm, kept_ref),
                (bias_hbm, bias_ref),
                (gain_hbm, gain_ref),
                (q_hbm, q_ref),
                (k_hbm, k_ref),
                (v_hbm, v_ref),
                (cot_hbm, cot_ref),
            )
        )
    ]
    for load in loads:
        load.start()
    barrier = pltpu.get_barrier_semaphore()

    @pl.loop(1, n)
    def _(j):
        pl.semaphore_signal(
            barrier, inc=1, device_id={"dp": lax.rem(me + j, n)}, device_id_type=MESH
        )

    @pl.loop(1, n_mp)
    def _(j):
        pl.semaphore_signal(
            barrier, inc=1, device_id={"mp": lax.rem(me_mp + j, n_mp)}, device_id_type=MESH
        )

    pl.semaphore_wait(barrier, n - 1 + n_mp - 1)

    near = n // 2
    side = me // near

    def each_peer(run):
        @pl.loop(0, near)
        def _(i):
            run((1 - side) * near + lax.rem(me + i, near))

        @pl.loop(1, near)
        def _(i):
            run(side * near + lax.rem(me + i, near))

    def guard(condition, run):
        if every:
            run()
        else:
            pl.when(condition)(run)

    def base(chunk):
        return 0 if every else chunk * members

    def is_member(chunk, device):
        return (device >= base(chunk)) & (device < base(chunk) + members)

    def window(ref, index):
        row = pl.multiple_of((index // col_groups) * rows, 16)
        if col_groups == 1:
            return ref.at[pl.ds(row, rows)]
        col = pl.multiple_of(lax.rem(index, col_groups) * width, LANES)
        return ref.at[pl.ds(row, rows), pl.ds(col, width)]

    chunks = ((mk_hbm, rx_k, st_k, mem_k), (mv_hbm, rx_v, st_v, mem_v))

    for c, (hbm, rx, st, mem) in enumerate(chunks):

        def first(dest):
            def send():
                pltpu.make_async_remote_copy(
                    src_ref=window(hbm, dest - base(c)),
                    dst_ref=rx.at[me],
                    send_sem=p1_send.at[c],
                    recv_sem=p1_recv.at[c],
                    device_id={"dp": dest},
                    device_id_type=MESH,
                ).start()

            guard(is_member(c, dest), send)

        each_peer(first)

        def own():
            pltpu.make_async_copy(
                window(hbm, me - base(c)), rx.at[me], p1_recv.at[c]
            ).start()

        guard(is_member(c, me), own)

    loads[0].wait()
    loads[1].wait()
    @pl.loop(0, n)
    def _(s):
        src_sm[s] = lax.fori_loop(
            0, n, lambda i, a: jnp.where(owner_ref[i] == s, i, a), jnp.int32(0)
        )

    kept_here = lax.fori_loop(
        0, n, lambda i, a: a + jnp.where(owner_ref[i] == me, kept_ref[i], 0), jnp.int32(0)
    )

    loads[2].wait()
    ki = lax.broadcasted_iota(jnp.int32, (pos_len, pos_len), 0)
    di = lax.broadcasted_iota(jnp.int32, (pos_len, pos_len), 1)
    total = ki + di
    flip = ((total == mem_len) | (total == mem_len + pos_len)).astype(jnp.float32)
    bias_pad = jnp.concatenate(
        [bias_ref[...], jnp.zeros((8 - heads, pos_len), jnp.float32)], axis=0
    )
    bias_rev = jnp.dot(bias_pad, flip, precision=HIGHEST, preferred_element_type=jnp.float32)

    qi = lax.broadcasted_iota(jnp.int32, (seg_len, seg_len), 0)
    ti = lax.broadcasted_iota(jnp.int32, (seg_len, seg_len), 1)
    causal = ti <= qi
    NT = (((1,), (1,)), ((), ()))
    TN = (((0,), (0,)), ((), ()))

    def cs(h):
        return slice(h * DH, (h + 1) * DH)

    def seg_scores(h):
        table = pltpu.roll(
            jnp.broadcast_to(bias_rev[h : h + 1], (seg_len, pos_len)),
            0,
            1,
            stride=1,
            stride_axis=0,
        )
        s = lax.dot_general(
            q_ref[:, cs(h)], k_ref[:, cs(h)], NT, preferred_element_type=jnp.float32
        )
        s = s * scale + table[:, mem_len:]
        prob[h, :, mem_len:] = jnp.where(causal, s, -1e30)
        prob[h, :, :mem_len] = table[:, :mem_len]

    def wait_first_and_forward(c):
        _, rx, st, mem = chunks[c]

        def run():
            pltpu.make_async_copy(rx, rx, p1_recv.at[c]).wait()

            @pl.loop(0, n)
            def _(s):
                st[s] = rx[src_sm[s]]

            def second(dest):
                pltpu.make_async_remote_copy(
                    src_ref=st.at[dest],
                    dst_ref=window(mem, me - base(c)),
                    send_sem=p2_send.at[c],
                    recv_sem=p2_recv.at[c],
                    device_id={"dp": dest},
                    device_id_type=MESH,
                ).start()

            each_peer(second)
            pltpu.make_async_copy(
                st.at[me], window(mem, me - base(c)), p2_recv.at[c]
            ).start()

        guard(is_member(c, me), run)

    for load in loads[3:]:
        load.wait()
    for h in range(heads):
        seg_scores(h)
    wait_first_and_forward(0)
    wait_first_and_forward(1)
    pltpu.make_async_copy(mem_k, mem_k, p2_recv.at[0]).wait()

    mi = lax.broadcasted_iota(jnp.int32, (seg_len, mem_len), 1)
    live = mi >= mem_len - BLOCK * kept_here
    for h in range(heads):
        s_mem = lax.dot_general(
            q_ref[:, cs(h)], mem_k[:, cs(h)], NT, preferred_element_type=jnp.float32
        )
        s_mem = jnp.where(live, s_mem * scale + prob[h, :, :mem_len], -1e30)
        s_seg = prob[h, :, mem_len:]
        row_max = jnp.maximum(
            jnp.max(s_mem, axis=1, keepdims=True), jnp.max(s_seg, axis=1, keepdims=True)
        )
        e_mem = jnp.where(live, jnp.exp(s_mem - row_max), 0.0)
        e_seg = jnp.where(causal, jnp.exp(s_seg - row_max), 0.0)
        norm = 1.0 / (
            jnp.sum(e_mem, axis=1, keepdims=True) + jnp.sum(e_seg, axis=1, keepdims=True)
        )
        p_seg = e_seg * norm
        prob[h, :, :mem_len] = e_mem * norm
        prob[h, :, mem_len:] = p_seg
        attn[:, cs(h)] = jnp.dot(
            p_seg.astype(jnp.bfloat16), v_ref[:, cs(h)], preferred_element_type=jnp.float32
        )

    pltpu.make_async_copy(mem_v, mem_v, p2_recv.at[1]).wait()

    squares = jnp.zeros((seg_len, DH), jnp.float32)
    crosses = jnp.zeros((seg_len, DH), jnp.float32)
    for h in range(heads):
        out = attn[:, cs(h)] + jnp.dot(
            prob[h, :, :mem_len].astype(jnp.bfloat16),
            mem_v[:, cs(h)],
            preferred_element_type=jnp.float32,
        )
        attn[:, cs(h)] = out
        squares = squares + out * out
        crosses = crosses + cot_ref[:, cs(h)].astype(jnp.float32) * gain_ref[cs(h)][None] * out
    lane = lax.broadcasted_iota(jnp.int32, (seg_len, DH), 1)
    both = jnp.where(
        lane == 0,
        jnp.sum(squares, axis=1, keepdims=True),
        jnp.sum(crosses, axis=1, keepdims=True),
    )
    mp_send[...] = jnp.transpose(both)[:8]

    @pl.loop(1, n_mp)
    def _(j):
        pltpu.make_async_remote_copy(
            src_ref=mp_send,
            dst_ref=mp_recv.at[me_mp],
            send_sem=mp_ssem,
            recv_sem=mp_rsem,
            device_id={"mp": lax.rem(me_mp + j, n_mp)},
            device_id_type=MESH,
        ).start()

    pltpu.make_async_copy(mp_send, mp_recv.at[me_mp], mp_rsem).start()
    pltpu.make_async_copy(mp_recv, mp_recv, mp_rsem).wait()
    sums = mp_recv[0]
    for m in range(1, n_mp):
        sums = sums + mp_recv[m]
    sums = jnp.transpose(
        jnp.concatenate([sums, jnp.zeros((LANES - 8, seg_len), jnp.float32)], axis=0)
    )
    inv_rms = lax.rsqrt(sums[:, 0:1] / HD + 1e-06)
    pull = inv_rms * inv_rms * inv_rms * sums[:, 1:2] / HD

    gain_rows, out_grads = [], []
    for h in range(heads):
        out = attn[:, cs(h)]
        gain = gain_ref[cs(h)][None]
        up = cot_ref[:, cs(h)].astype(jnp.float32)
        normed = out * inv_rms
        att_ref[:, cs(h)] = (normed * gain).astype(jnp.bfloat16)
        gain_rows.append(jnp.sum(up * normed, axis=0, keepdims=True))
        og = (inv_rms * (up * gain) - out * pull).astype(jnp.bfloat16)
        delta = jnp.sum(og.astype(jnp.float32) * out, axis=1, keepdims=True)
        p_mem = prob[h, :, :mem_len]
        p_seg = prob[h, :, mem_len:]
        g_mem = p_mem * (
            lax.dot_general(og, mem_v[:, cs(h)], NT, preferred_element_type=jnp.float32) - delta
        )
        g_seg = p_seg * (
            lax.dot_general(og, v_ref[:, cs(h)], NT, preferred_element_type=jnp.float32) - delta
        )
        grads[h, :, :mem_len] = g_mem.astype(jnp.bfloat16)
        grads[h, :, mem_len:] = g_seg.astype(jnp.bfloat16)
        out_grads.append(og)
        x = jnp.concatenate([g_mem, g_seg], axis=1)
        half = seg_len // 2
        while half >= 8:
            x = x[:half] + pltpu.roll(x[half:], pos_len - half, 1)
            half //= 2
        folded[h * 8 : (h + 1) * 8] = x

    x = folded[...]
    for half in (4, 2, 1):
        x = x + pltpu.roll(pltpu.roll(x, pos_len - half, 1), heads * 8 - half, 0)
    rows8 = [x[8 * h : 8 * h + 1] for h in range(heads)]
    rows8.append(jnp.zeros((8 - heads, pos_len), jnp.float32))
    diag[...] = jnp.dot(
        jnp.concatenate(rows8, axis=0), flip, precision=HIGHEST, preferred_element_type=jnp.float32
    )
    gain_block = jnp.concatenate(
        gain_rows + [jnp.zeros((8 - heads, DH), jnp.float32)], axis=0
    )
    for b in range(pos_len // LANES):
        pkt[b, :8] = diag[:, b * LANES : (b + 1) * LANES]
        pkt[b, 8:] = gain_block

    part = pos_len // n

    def packet(dest):
        pltpu.make_async_remote_copy(
            src_ref=pkt.at[(dest * part) // LANES],
            dst_ref=pkt_recv.at[me],
            send_sem=dp_ssem,
            recv_sem=dp_rsem,
            device_id={"dp": dest},
            device_id_type=MESH,
        ).start()

    each_peer(packet)
    pltpu.make_async_copy(pkt.at[(me * part) // LANES], pkt_recv.at[me], dp_rsem).start()

    stores = [
        pltpu.make_async_copy(a, b, out_sem.at[i])
        for i, (a, b) in enumerate(
            ((att_ref, att_hbm), (dv_ref, dv_hbm), (dk_ref, dk_hbm), (dq_ref, dq_hbm))
        )
    ]
    stores[0].start()
    for h in range(heads):
        dv = lax.dot_general(
            prob[h, :, mem_len:].astype(jnp.bfloat16),
            out_grads[h],
            TN,
            preferred_element_type=jnp.float32,
        )
        dv_ref[:, cs(h)] = dv.astype(jnp.bfloat16)
    stores[1].start()
    for h in range(heads):
        dk = lax.dot_general(
            grads[h, :, mem_len:], q_ref[:, cs(h)], TN, preferred_element_type=jnp.float32
        )
        dk_ref[:, cs(h)] = (dk * scale).astype(jnp.bfloat16)
    stores[2].start()
    for h in range(heads):
        dq = jnp.dot(
            grads[h, :, :mem_len], mem_k[:, cs(h)], preferred_element_type=jnp.float32
        ) + jnp.dot(grads[h, :, mem_len:], k_ref[:, cs(h)], preferred_element_type=jnp.float32)
        dq_ref[:, cs(h)] = (dq * scale).astype(jnp.bfloat16)
    stores[3].start()

    for c, (hbm, rx, st, mem) in enumerate(chunks):

        def wait_p1(count):
            pltpu.make_async_copy(
                rx.at[pl.ds(0, count)], rx.at[pl.ds(0, count)], p1_send.at[c]
            ).wait()

        def wait_p2():
            pltpu.make_async_copy(
                st.at[pl.ds(0, n - 1)], st.at[pl.ds(0, n - 1)], p2_send.at[c]
            ).wait()

        guard(is_member(c, me), functools.partial(wait_p1, members - 1))
        if not every:
            pl.when(jnp.logical_not(is_member(c, me)))(functools.partial(wait_p1, members))
        guard(is_member(c, me), wait_p2)
    pltpu.make_async_copy(
        mp_recv.at[pl.ds(0, n_mp - 1)], mp_recv.at[pl.ds(0, n_mp - 1)], mp_ssem
    ).wait()

    pltpu.make_async_copy(pkt_recv, pkt_recv, dp_rsem).wait()
    acc = pkt_recv[0]
    for s in range(1, n):
        acc = acc + pkt_recv[s]
    offset = lax.rem(me * part, LANES)
    mine = pltpu.roll(acc[:8], lax.rem(LANES - offset, LANES), 1)
    dbias_ref[...] = mine[:heads, :part]
    for h in range(heads):
        dgain_ref[cs(h)] = acc[8 + h]
    for store in stores:
        store.wait()
    pltpu.make_async_copy(
        pkt_recv.at[pl.ds(0, n - 1)], pkt_recv.at[pl.ds(0, n - 1)], dp_ssem
    ).wait()


def hand_on(*refs):
    count = (len(refs) - 2) // 3
    given, taken, held = refs[:count], refs[count : 2 * count], refs[2 * count : 3 * count]
    in_sem, out_sem = refs[-2:]
    loads = [
        pltpu.make_async_copy(given[i], held[i], in_sem.at[i]) for i in range(count)
    ]
    stores = [
        pltpu.make_async_copy(held[i], taken[i], out_sem.at[i]) for i in range(count)
    ]
    for load in loads:
        load.start()
    for load, store in zip(loads, stores):
        load.wait()
        store.start()
    for store in stores:
        store.wait()


def body(
    n,
    n_mp,
    seg_queries,
    seg_keys,
    seg_values,
    memory_keys,
    memory_values,
    new_owner,
    kept_blocks,
    rel_bias,
    norm_gain,
    cotangent,
):
    _, seg_len, cols = seg_queries.shape
    mem_len = memory_keys.shape[1]
    heads, pos_len = rel_bias.shape
    part = pos_len // n
    plan = share_plan(n, mem_len, cols)
    members, rows, width, _ = plan
    bf16, f32 = jnp.bfloat16, jnp.float32
    vmem = pl.BlockSpec(memory_space=pltpu.VMEM)
    hbm = pl.BlockSpec(memory_space=pltpu.HBM)
    big = jax.ShapeDtypeStruct((seg_len, cols), bf16)
    outs = pl.pallas_call(
        functools.partial(kernel, n, n_mp, plan),
        out_shape=(
            big,
            big,
            big,
            big,
            jax.ShapeDtypeStruct((heads, part), f32),
            jax.ShapeDtypeStruct((cols,), f32),
        ),
        in_specs=[hbm] * 10,
        out_specs=(hbm,) * 4 + (vmem,) * 2,
        scratch_shapes=[
            pltpu.VMEM((seg_len, cols), bf16),
            pltpu.VMEM((seg_len, cols), bf16),
            pltpu.VMEM((seg_len, cols), bf16),
            pltpu.VMEM((heads, pos_len), f32),
            pltpu.VMEM((seg_len, cols), bf16),
            pltpu.VMEM((cols,), f32),
            pltpu.SMEM((n,), jnp.int32),
            pltpu.SMEM((n,), jnp.int32),
            pltpu.VMEM((seg_len, cols), bf16),
            pltpu.VMEM((seg_len, cols), bf16),
            pltpu.VMEM((seg_len, cols), bf16),
            pltpu.VMEM((seg_len, cols), bf16),
            pltpu.VMEM((heads, seg_len, pos_len), bf16),
            pltpu.SemaphoreType.DMA((9,)),
            pltpu.SemaphoreType.DMA((4,)),
            pltpu.VMEM((n, rows, width), bf16),
            pltpu.VMEM((n, rows, width), bf16),
            pltpu.VMEM((n, rows, width), bf16),
            pltpu.VMEM((n, rows, width), bf16),
            pltpu.VMEM((mem_len, cols), bf16),
            pltpu.VMEM((mem_len, cols), bf16),
            pltpu.SMEM((n,), jnp.int32),
            pltpu.VMEM((heads, seg_len, pos_len), f32),
            pltpu.VMEM((seg_len, cols), f32),
            pltpu.VMEM((8, seg_len), f32),
            pltpu.VMEM((n_mp, 8, seg_len), f32),
            pltpu.VMEM((heads * 8, pos_len), f32),
            pltpu.VMEM((8, pos_len), f32),
            pltpu.VMEM((pos_len // LANES, 16, LANES), f32),
            pltpu.VMEM((n, 16, LANES), f32),
            pltpu.SemaphoreType.DMA((2,)),
            pltpu.SemaphoreType.DMA((2,)),
            pltpu.SemaphoreType.DMA((2,)),
            pltpu.SemaphoreType.DMA((2,)),
            pltpu.SemaphoreType.DMA,
            pltpu.SemaphoreType.DMA,
            pltpu.SemaphoreType.DMA,
            pltpu.SemaphoreType.DMA,
        ],
        compiler_params=pltpu.CompilerParams(
            collective_id=0, has_side_effects=True, vmem_limit_bytes=60 * 1024 * 1024
        ),
    )(
        new_owner,
        kept_blocks,
        seg_queries[0],
        seg_keys[0],
        seg_values[0],
        memory_keys[0],
        memory_values[0],
        rel_bias,
        norm_gain,
        cotangent[0],
    )
    final = pl.pallas_call(
        hand_on,
        out_shape=tuple(jax.ShapeDtypeStruct(o.shape, o.dtype) for o in outs),
        in_specs=[hbm] * 6,
        out_specs=(hbm,) * 6,
        scratch_shapes=[pltpu.VMEM(o.shape, o.dtype) for o in outs]
        + [pltpu.SemaphoreType.DMA((6,)), pltpu.SemaphoreType.DMA((6,))],
        compiler_params=pltpu.CompilerParams(vmem_limit_bytes=60 * 1024 * 1024),
    )(*outs)
    return (
        final[0][None],
        final[1][None],
        final[2][None],
        final[3][None],
        final[4],
        final[5],
    )


def solution(mesh):
    rows = P("dp", None, "mp")
    in_specs = (rows, rows, rows, rows, rows, P(), P(), P("mp", None), P("mp"), rows)
    out_specs = (rows, rows, rows, rows, P("mp", "dp"), P("mp"))
    return jax.shard_map(
        functools.partial(body, mesh.shape["dp"], mesh.shape["mp"]),
        mesh=mesh,
        in_specs=in_specs,
        out_specs=out_specs,
        check_vma=False,
    )
```
